128 devices in a mesh: dp: 2 (over x_hi), ctx: 64 (over y, x_lo, z, core).
Axes of the slice: x: 4 (x_hi: 2, x_lo: 2; x = x_hi * 2 + x_lo), y: 4, z: 4, core: 2. Of those that a mesh axis runs over, the one named last changes fastest.
Arguments:
- queries: bfloat16 [40960, 3072], P(('dp', 'ctx')), parts along dimension 0, may hold values from -300 to 300
- latent: bfloat16 [40960, 576], P(('dp', 'ctx')), parts along dimension 0, may hold values from -4 to 4
- w_key_up: bfloat16 [512, 2048], replicated, may hold values from -0.25 to 0.25
- w_value_up: bfloat16 [512, 2048], replicated, may hold values from -0.25 to 0.25
- grad_out: bfloat16 [40960, 2048], P(('dp', 'ctx')), parts along dimension 0, may hold values from -6 to 6
- span_order: int32 [256], P('dp'), parts along dimension 0, may hold values from 0 to 127, each once
Outputs:
- attn_out: bfloat16 [40960, 2048], P(('dp', 'ctx')), parts along dimension 0
- grad_queries: bfloat16 [40960, 3072], P(('dp', 'ctx')), parts along dimension 0
- grad_latent: bfloat16 [40960, 576], P(('dp', 'ctx')), parts along dimension 0
The draws below stay inside these ranges and needn't reach their ends.
There are 2 independent parts, one for each index of `dp`. The reference program is written for one: setup_inputs(seed, part) draws one part's arguments, and reference() takes and returns one part's arrays. A program takes and returns all parts, laid end to end along the dimension named above; an argument that names none is the same for every part. Nothing has to cross between parts.
Inputs may be any that keep to these rules, and one draw needn't show every extreme that they name: `span_order`: each block number appears once.
All inputs are finite; a program needn't handle non-finite values.
Results may differ from the reference program's by a relative error of at most 0.0083.
Values may be sent and summed in bfloat16 or wider, within the bound.
No kernel may reach another device: no remote copies, remote signals or barrier semaphores. Data moves between devices by JAX's collectives and lax.ppermute only.
A program may use at most 192 MiB of HBM per device.

```python
import jax
import jax.numpy as jnp
from jax import lax

HEADS = 16
NOPE = 128
ROPE = 64
VDIM = 128
LATENT = 512
TOK_DEV = 320
SPAN = 160
TOKENS = 20480
N_CTX = 64


def rope_rows(key):
    return jax.random.truncated_normal(key, -4.0, 4.0, (TOKENS, ROPE), jnp.float32)


def draw_latent(key, part):
    rotary = rope_rows(key)
    key = jax.random.fold_in(key, 11)
    content = jax.random.truncated_normal(key, -4.0, 4.0, (TOKENS, LATENT), jnp.float32)
    return jnp.concatenate([content, rotary], 1).astype(jnp.bfloat16)


def draw_queries(key, part):
    key = jax.random.fold_in(key, 23)
    content = jax.random.truncated_normal(key, -4.0, 4.0, (TOKENS, HEADS, NOPE + ROPE), jnp.float32)
    return content.reshape(TOKENS, -1).astype(jnp.bfloat16)


def level_of(own_key, shape, cuts, smallest, largest):
    def one(position, shards_of):
        steps = jax.random.uniform(jax.random.fold_in(jax.random.fold_in(own_key, 6), position), (shards_of,), jnp.float32, smallest / len(cuts), largest / len(cuts))
        return jnp.repeat(jnp.exp(steps), shape[position] // shards_of).reshape((-1,) + (1,) * (len(shape) - position - 1))

    level = one(*cuts[0])
    for cut in cuts[1:]:
        level = level * one(*cut)
    return level


def centred(key, dims, deviation, bound, pieces=(), kind=jnp.bfloat16):
    result = jax.random.normal(key, dims, jnp.float32) * deviation
    if len(pieces) > 0:
        result = level_of(key, dims, pieces, -0.22, 0.18) * result
    return jnp.clip(result, min=-bound, max=bound).astype(kind)


def setup_inputs(seed: int = 0, part: int = 0) -> dict:
    key_list = jax.random.split(jax.random.key(seed), 7)
    own_keys = jax.random.split(jax.random.fold_in(key_list[6], part), 7)
    return {
        "queries": draw_queries(jax.random.fold_in(jax.random.fold_in(key_list[6], part), 71), part),
        "latent": draw_latent(jax.random.fold_in(jax.random.fold_in(key_list[6], part), 71), part),
        "w_key_up": centred(key_list[2], (LATENT, HEADS * NOPE), LATENT ** -0.5, 0.25),
        "w_value_up": centred(key_list[3], (LATENT, HEADS * VDIM), LATENT ** -0.5, 0.25),
        "grad_out": centred(own_keys[4], (TOKENS, HEADS * VDIM), 1.0, 6.0, ((0, 64),)),
        "span_order": jax.random.permutation(own_keys[5], 2 * N_CTX).astype(jnp.int32),
    }


def attend_blocks(query_rows, key_nope, key_rope, value_rows, cotangent, allowed, w_key_up, w_value_up):
    highest = lax.Precision.HIGHEST
    query_count = query_rows.shape[0]
    key_count = key_nope.shape[0]
    heads = key_nope.shape[1]
    nope = key_nope.shape[2]
    query_heads = query_rows.reshape(query_count, heads, -1).astype(jnp.float32)
    scale = query_heads.shape[2] ** -0.5
    query_nope = query_heads[..., :nope]
    query_rope = query_heads[..., nope:]
    knope = key_nope.astype(jnp.float32)
    krope = key_rope.astype(jnp.float32)
    vals = value_rows.astype(jnp.float32)
    scores = (jnp.einsum('qhd,khd->hqk', query_nope, knope, precision=highest)
              + jnp.einsum('qhd,kd->hqk', query_rope, krope, precision=highest)) * scale
    scores = jnp.where(allowed[None], scores, -jnp.inf)
    highest_score = jnp.max(scores, -1, keepdims=True)
    expo = jnp.exp(scores - highest_score)
    probs = expo / jnp.sum(expo, -1, keepdims=True)
    probs_low = lax.optimization_barrier(probs.astype(jnp.bfloat16)).astype(jnp.float32)
    output = jnp.einsum('hqk,khd->qhd', probs_low, vals, precision=highest).astype(jnp.bfloat16)
    grad_heads = cotangent.reshape(query_count, heads, -1).astype(jnp.float32)
    dprobs = jnp.einsum('qhd,khd->hqk', grad_heads, vals, precision=highest)
    delta = jnp.sum(probs * dprobs, -1, keepdims=True)
    dscores = lax.optimization_barrier((probs * (dprobs - delta)).astype(jnp.bfloat16)).astype(jnp.float32)
    dquery_nope = jnp.einsum('hqk,khd->qhd', dscores, knope, precision=highest) * scale
    dquery_rope = jnp.einsum('hqk,kd->qhd', dscores, krope, precision=highest) * scale
    dquery = jnp.concatenate([dquery_nope, dquery_rope], -1).reshape(query_count, -1).astype(jnp.bfloat16)
    dkey_nope = (jnp.einsum('hqk,qhd->khd', dscores, query_nope, precision=highest) * scale).astype(jnp.bfloat16)
    dkey_rope = jnp.einsum('hqk,qhd->kd', dscores, query_rope, precision=highest) * scale
    dvalues = jnp.einsum('hqk,qhd->khd', probs_low, grad_heads, precision=highest).astype(jnp.bfloat16)
    dlatent = (jnp.dot(dkey_nope.reshape(key_count, -1), w_key_up.T, preferred_element_type=jnp.float32)
               + jnp.dot(dvalues.reshape(key_count, -1), w_value_up.T, preferred_element_type=jnp.float32))
    term = jnp.concatenate([dlatent, dkey_rope], -1)
    return output.reshape(query_count, -1), dquery, term


def reference(queries, latent, w_key_up, w_value_up, grad_out, span_order):
    cycle_size = N_CTX
    tok_count = TOK_DEV
    span_len = SPAN
    latent_part = latent[:, :LATENT]
    key_all = jnp.dot(latent_part, w_key_up, preferred_element_type=jnp.float32).astype(jnp.bfloat16)
    key_all = key_all.reshape(cycle_size, tok_count, HEADS, NOPE)
    value_all = jnp.dot(latent_part, w_value_up, preferred_element_type=jnp.float32).astype(jnp.bfloat16)
    value_all = value_all.reshape(cycle_size, tok_count, HEADS, VDIM)
    rope_all = latent[:, LATENT:].reshape(cycle_size, tok_count, ROPE)
    query_all = queries.reshape(cycle_size, tok_count, -1)
    grad_all = grad_out.reshape(cycle_size, tok_count, -1)
    offsets = jnp.arange(tok_count, dtype=jnp.int32)
    order_pairs = span_order.reshape(cycle_size, 2).astype(jnp.int32)
    pos_all = order_pairs[:, offsets // span_len] * span_len + offsets % span_len

    def per_device(owner):
        sources = ((owner - jnp.arange(3, dtype=jnp.int32)) % cycle_size).astype(jnp.int32)
        key_nope = key_all[sources].reshape(3 * tok_count, HEADS, NOPE)
        value_rows = value_all[sources].reshape(3 * tok_count, HEADS, VDIM)
        key_rope = rope_all[sources].reshape(3 * tok_count, ROPE)
        key_pos = pos_all[sources].reshape(-1)
        allowed = key_pos[None, :] <= pos_all[owner][:, None]
        return attend_blocks(query_all[owner], key_nope, key_rope, value_rows, grad_all[owner],
                             allowed, w_key_up, w_value_up)

    outputs, dqueries, terms = lax.map(per_device, jnp.arange(cycle_size, dtype=jnp.int32))
    terms = terms.reshape(cycle_size, 3, tok_count, LATENT + ROPE)
    total = terms[:, 0] + jnp.roll(terms[:, 1], -1, 0) + jnp.roll(terms[:, 2], -2, 0)
    return (outputs.reshape(TOKENS, -1), dqueries.reshape(TOKENS, -1),
            total.reshape(TOKENS, -1).astype(jnp.bfloat16))
```

```python
import jax
import jax.numpy as jnp
from jax import lax
from jax.experimental import pallas as pl
from jax.experimental.pallas import tpu as pltpu
from jax.sharding import PartitionSpec as P
HEADS=16; NOPE=128; ROPE=64; VDIM=128; LATENT=512; DQ=192
SCALE=DQ**-0.5
C2=SCALE*1.4426950408889634
NEG=-1e30
NT=(((1,),(1,)),((),()))
TN=(((0,),(0,)),((),()))
F32=jnp.float32; BF=jnp.bfloat16

def body(spans, q_ref, do_ref, own, near, far, wk_ref, wv_ref, out_ref, dq_ref, t_ref, bias, lat, rope, accT, ropeT):
    p=pl.program_id(0)
    T=q_ref.shape[0]; W=3*T; H=T//2
    @pl.when(p==0)
    def _():
        lat[0:T]=own[:, :LATENT]; lat[T:2*T]=near[:, :LATENT]; lat[2*T:]=far[:, :LATENT]
        rope[0:T]=own[:, LATENT:]; rope[T:2*T]=near[:, LATENT:]; rope[2*T:]=far[:, LATENT:]
        col=lax.broadcasted_iota(jnp.int32,(1,W),1)
        kp=jnp.full((1,W),spans[5]*H-5*H,jnp.int32)
        for j in range(4,-1,-1):
            kp=jnp.where(col<(j+1)*H, spans[j]*H-j*H, kp)
        kp=kp+col
        row=lax.broadcasted_iota(jnp.int32,(T,1),0)
        qp=jnp.where(row<H, spans[0]*H, spans[1]*H-H)+row
        bias[...]=jnp.where(kp<=qp,0.0,NEG).astype(F32)
        accT[...]=jnp.zeros_like(accT); ropeT[...]=jnp.zeros_like(ropeT)
    outs=[];dqs=[];dks=[];dvs=[]; rt=None
    for h in range(2):
        q=q_ref[:, h*DQ:(h+1)*DQ]
        do=do_ref[:, h*VDIM:(h+1)*VDIM]
        w=jnp.concatenate([wk_ref[:, h*128:(h+1)*128], wv_ref[:, h*128:(h+1)*128]],1)
        kv=jnp.dot(lat[...],w,preferred_element_type=F32).astype(BF)
        k=jnp.concatenate([kv[:, :128],rope[...]],1)
        v=kv[:,128:]
        s=lax.dot_general(q,k,NT,preferred_element_type=F32)+bias[...]
        m=jnp.max(s,1,keepdims=True)
        e=jnp.exp2((s-m)*C2).astype(BF)
        va=jnp.concatenate([v,jnp.ones_like(v)],1)
        oa=jnp.dot(e,va,preferred_element_type=F32)
        rl=1.0/oa[:,128:]
        out=oa[:,:128]*rl
        dof=do.astype(F32)
        delta=jnp.sum(out*dof,1,keepdims=True)
        dp=lax.dot_general(do,v,NT,preferred_element_type=F32)
        ds=(e.astype(F32)*(dp-delta)).astype(BF)
        rs=rl[:, :1]*SCALE
        dq=jnp.dot(ds,k,preferred_element_type=F32)*rs
        qs=(q.astype(F32)*rs).astype(BF)
        dos=(dof*rl).astype(BF)
        dk=lax.dot_general(qs,ds,TN,preferred_element_type=F32)
        dv=lax.dot_general(dos,e,TN,preferred_element_type=F32)
        outs.append(out.astype(BF)); dqs.append(dq.astype(BF))
        dks.append(dk[:128].astype(BF)); dvs.append(dv.astype(BF))
        rt=dk[128:] if rt is None else rt+dk[128:]
    out_ref[...]=jnp.concatenate(outs,1)
    dq_ref[...]=jnp.concatenate(dqs,1)
    ropeT[...]+=rt
    wcat=jnp.concatenate([wk_ref[...],wv_ref[...]],1)
    d=jnp.concatenate(dks+dvs,0)
    accT[...]+=jnp.dot(wcat,d,preferred_element_type=F32)
    @pl.when(p==pl.num_programs(0)-1)
    def _():
        t_ref[:, :LATENT]=accT[...].T
        t_ref[:, LATENT:]=ropeT[...].T

def fused(spans,q,do,own,near,far,wk,wv):
    T=q.shape[0]
    full=lambda a: pl.BlockSpec(a.shape,lambda p,s:(0,0))
    col=lambda n: pl.BlockSpec((T,n),lambda p,s:(0,p))
    wsp=pl.BlockSpec((LATENT,256),lambda p,s:(0,p))
    return pl.pallas_call(body,
        grid_spec=pltpu.PrefetchScalarGridSpec(num_scalar_prefetch=1,grid=(HEADS//2,),
          in_specs=[col(384),col(256),full(own),full(near),full(far),wsp,wsp],
          out_specs=[col(256),col(384),pl.BlockSpec((3*T,576),lambda p,s:(0,0))],
          scratch_shapes=[pltpu.VMEM((T,3*T),F32),pltpu.VMEM((3*T,LATENT),BF),pltpu.VMEM((3*T,ROPE),BF),pltpu.VMEM((LATENT,3*T),F32),pltpu.VMEM((ROPE,3*T),F32)]),
        out_shape=[jax.ShapeDtypeStruct((T,2048),BF),jax.ShapeDtypeStruct((T,3072),BF),jax.ShapeDtypeStruct((3*T,576),F32)],
        compiler_params=pltpu.CompilerParams(vmem_limit_bytes=56*2**20,dimension_semantics=("arbitrary",)),
    )(spans,q,do,own,near,far,wk,wv)


def shifted(block, distance):
    n=lax.axis_size("ctx")
    return lax.ppermute(block,"ctx",[((i-distance)%n,i) for i in range(n)])

def on_device(queries, latent, w_key_up, w_value_up, grad_out, span_order):
    n=lax.axis_size("ctx"); me=lax.axis_index("ctx"); T=queries.shape[0]
    near=shifted(latent,1); far=shifted(latent,2)
    pairs=span_order.reshape(n,2)
    spans=jnp.concatenate([pairs[(me-d)%n] for d in range(3)])
    out,dq,t=fused(spans,queries,grad_out,latent,near,far,w_key_up,w_value_up)
    a=shifted(t[T:2*T].astype(BF),-1); b=shifted(t[2*T:].astype(BF),-2)
    total=t[:T]+a.astype(F32)+b.astype(F32)
    return out,dq,total.astype(BF)

def solution(mesh):
    rows=P(("dp","ctx"),None)
    return jax.shard_map(on_device,mesh=mesh,in_specs=(rows,rows,P(),P(),rows,P("dp")),out_specs=(rows,rows,rows),check_vma=False)
```

```python
import jax
import jax.numpy as jnp
from jax import lax
from jax.experimental import pallas as pl
from jax.experimental.pallas import tpu as pltpu
from jax.sharding import PartitionSpec as P

HEADS = 16
NOPE = 128
ROPE = 64
VDIM = 128
LATENT = 512
DQ = NOPE + ROPE
SCALE = DQ**-0.5
EXP2_SCALE = SCALE * 1.4426950408889634
MASKED = -1e30
NT = (((1,), (1,)), ((), ()))
TN = (((0,), (0,)), ((), ()))
F32 = jnp.float32
BF = jnp.bfloat16


def dot(x, y):
    return jnp.dot(x, y, preferred_element_type=F32)


def dot_rows(x, y):
    half = x.shape[0] // 2
    return jnp.concatenate([dot(x[:half], y), dot(x[half:], y)], 0)


def dot_nt(x, y):
    return lax.dot_general(x, y, NT, preferred_element_type=F32)


def dot_tn(x, y):
    return lax.dot_general(x, y, TN, preferred_element_type=F32)


def q_head(ref, h):
    return ref[:, h * DQ : (h + 1) * DQ]


def v_head(ref, h):
    return ref[:, h * VDIM : (h + 1) * VDIM]


def head_weights(wk_ref, wv_ref, h):
    return jnp.concatenate([v_head(wk_ref, h), v_head(wv_ref, h)], 1)


def positions(rows, spans):
    half = rows // 2
    last = len(spans) - 1
    col = lax.broadcasted_iota(jnp.int32, (1, half * len(spans)), 1)
    base = jnp.full(col.shape, (spans[last] - last) * half, jnp.int32)
    for j in range(last - 1, -1, -1):
        base = jnp.where(col < (j + 1) * half, (spans[j] - j) * half, base)
    return base + col


def own_keys(own, wk_ref, wv_ref, kv_ref):
    for h in range(2):
        kv_ref[h] = dot_rows(own[:, :LATENT], head_weights(wk_ref, wv_ref, h)).astype(BF)


def main_body(spans, q_ref, do_ref, own, near, far, wk_ref, wv_ref, okv_ref,
              out_ref, ds_ref, oe_ref, k_ref, dos_ref, tn_ref, tf_ref, bias, acc_t, rope_t):
    p = pl.program_id(0)
    rows = q_ref.shape[0]
    half = rows // 2
    width = 2 * rows
    others = [spans[j] for j in range(2, 6)]
    pair = [spans[0], spans[1]]

    @pl.when(p == 0)
    def _():
        row = lax.broadcasted_iota(jnp.int32, (rows, 1), 0)
        q_pos = jnp.where(row < half, pair[0] * half, (pair[1] - 1) * half) + row
        bias[...] = jnp.where(positions(rows, pair) <= q_pos, 0.0, MASKED).astype(F32)
        acc_t[...] = jnp.zeros_like(acc_t)
        rope_t[...] = jnp.zeros_like(rope_t)

    other_pos = positions(rows, others)
    other_bias = [jnp.where(other_pos < pair[j] * half, 0.0, MASKED).astype(F32) for j in range(2)]
    rope = jnp.concatenate([near[:, LATENT:], far[:, LATENT:], own[:, LATENT:]], 0)

    def project(h):
        w = head_weights(wk_ref, wv_ref, h)
        kv = jnp.concatenate(
            [dot(near[:, :LATENT], w).astype(BF), dot(far[:, :LATENT], w).astype(BF), okv_ref[h]], 0
        )
        k = kv[:, :NOPE]
        k_ref[h] = k
        return jnp.concatenate([k, rope], 1), kv[:, NOPE:]

    def score(h, k):
        return dot_nt(q_head(q_ref, h), k)

    def soften(s):
        upper = s[:half, :width] + other_bias[0]
        lower = s[half:, :width] + other_bias[1]
        s = jnp.concatenate([jnp.concatenate([upper, lower], 0), s[:, width:] + bias[...]], 1)
        top = jnp.max(s, 1, keepdims=True)
        return jnp.exp2((s - top) * EXP2_SCALE).astype(BF)

    def attend(h, e, v):
        oe_ref[h] = e[:, width:]
        both = dot_rows(e, jnp.concatenate([v, jnp.ones_like(v)], 1))
        inv = 1.0 / both[:, VDIM:]
        out = both[:, :VDIM] * inv
        out_ref[:, h * VDIM : (h + 1) * VDIM] = out.astype(BF)
        dos = (v_head(do_ref, h).astype(F32) * inv).astype(BF)
        dos_ref[:, h * VDIM : (h + 1) * VDIM] = dos
        return dos, jnp.sum(out * dos.astype(F32), 1, keepdims=True)

    def dscores(h, e, dp, delta):
        ds = (e.astype(F32) * (dp - delta)).astype(BF)
        ds_ref[h] = ds
        return ds

    k0, v0 = project(0)
    s0 = score(0, k0)
    k1, v1 = project(1)
    e0 = soften(s0)
    s1 = score(1, k1)
    dos0, delta0 = attend(0, e0, v0)
    e1 = soften(s1)
    dp0 = dot_nt(dos0, v0)
    dos1, delta1 = attend(1, e1, v1)
    ds0 = dscores(0, e0, dp0, delta0)
    dp1 = dot_nt(dos1, v1)
    dv0 = dot_tn(dos0, e0[:, :width])
    dk0 = dot_tn(q_head(q_ref, 0), ds0[:, :width]) * SCALE
    ds1 = dscores(1, e1, dp1, delta1)
    dv1 = dot_tn(dos1, e1[:, :width])
    dk1 = dot_tn(q_head(q_ref, 1), ds1[:, :width]) * SCALE
    rope_t[...] += dk0[NOPE:] + dk1[NOPE:]
    w = jnp.concatenate([wk_ref[...], wv_ref[...]], 1)
    d = jnp.concatenate([dk0[:NOPE].astype(BF), dk1[:NOPE].astype(BF), dv0.astype(BF), dv1.astype(BF)], 0)
    acc_t[...] += dot(w, d)

    @pl.when(p == pl.num_programs(0) - 1)
    def _():
        tn_ref[:, :LATENT] = acc_t[:, :rows].astype(BF).T
        tn_ref[:, LATENT:] = rope_t[:, :rows].astype(BF).T
        tf_ref[:, :LATENT] = acc_t[:, rows:].astype(BF).T
        tf_ref[:, LATENT:] = rope_t[:, rows:].astype(BF).T


def tail_body(q_ref, dos_ref, own, near, far, wk_ref, wv_ref, ds_ref, oe_ref, k_ref,
              dq_ref, t_ref, acc_t, rope_t):
    p = pl.program_id(0)
    rows = q_ref.shape[0]
    width = 2 * rows

    @pl.when(p == 0)
    def _():
        acc_t[...] = jnp.zeros_like(acc_t)
        rope_t[...] = jnp.zeros_like(rope_t)

    rope = jnp.concatenate([near[:, LATENT:], far[:, LATENT:], own[:, LATENT:]], 0)
    dqs, dks, dvs, rope_sum = [], [], [], None
    for h in range(2):
        ds = ds_ref[h]
        dv = dot_tn(v_head(dos_ref, h), oe_ref[h])
        dk = dot_tn(q_head(q_ref, h), ds[:, width:]) * SCALE
        dq = dot_rows(ds, jnp.concatenate([k_ref[h], rope], 1)) * SCALE
        dqs.append(dq.astype(BF))
        dks.append(dk[:NOPE].astype(BF))
        dvs.append(dv.astype(BF))
        rope_sum = dk[NOPE:] if rope_sum is None else rope_sum + dk[NOPE:]
    dq_ref[...] = jnp.concatenate(dqs, 1)
    rope_t[...] += rope_sum
    w = jnp.concatenate([wk_ref[...], wv_ref[...]], 1)
    acc_t[...] += dot(w, jnp.concatenate(dks + dvs, 0))

    @pl.when(p == pl.num_programs(0) - 1)
    def _():
        t_ref[:, :LATENT] = acc_t[...].T
        t_ref[:, LATENT:] = rope_t[...].T


def whole(a):
    return pl.BlockSpec(a.shape, lambda p, *_: (0, 0))


def columns(rows, n):
    return pl.BlockSpec((rows, n), lambda p, *_: (0, p))


def pairs(rows, n):
    return pl.BlockSpec((2, rows, n), lambda p, *_: (p, 0, 0))


def params():
    return pltpu.CompilerParams(vmem_limit_bytes=48 * 2**20, dimension_semantics=("arbitrary",))


def cost(macs, size):
    return pl.CostEstimate(flops=2 * macs, bytes_accessed=size, transcendentals=0)


def shape(*dims, dtype=BF):
    return jax.ShapeDtypeStruct(dims, dtype)


def call_own_keys(own, wk, wv):
    rows = own.shape[0]
    return pl.pallas_call(
        own_keys,
        grid=(HEADS // 2,),
        in_specs=[whole(own), columns(LATENT, 256), columns(LATENT, 256)],
        out_specs=pairs(rows, 256),
        out_shape=shape(HEADS, rows, 256),
        compiler_params=params(),
        cost_estimate=cost(7 * 10**8, 8 * 10**6),
        name="own_keys",
    )(own, wk, wv)


def call_main(spans, q, do, own, near, far, wk, wv, okv):
    rows = q.shape[0]
    keys = 3 * rows
    return pl.pallas_call(
        main_body,
        grid_spec=pltpu.PrefetchScalarGridSpec(
            num_scalar_prefetch=1,
            grid=(HEADS // 2,),
            in_specs=[columns(rows, 2 * DQ), columns(rows, 2 * VDIM), whole(own), whole(near), whole(far),
                      columns(LATENT, 256), columns(LATENT, 256), pairs(rows, 256)],
            out_specs=[columns(rows, 2 * VDIM), pairs(rows, keys), pairs(rows, rows), pairs(keys, NOPE),
                       columns(rows, 2 * VDIM), whole(near), whole(far)],
            scratch_shapes=[
                pltpu.VMEM((rows, rows), F32),
                pltpu.VMEM((LATENT, 2 * rows), F32),
                pltpu.VMEM((ROPE, 2 * rows), F32),
            ],
        ),
        out_shape=[
            shape(*do.shape),
            shape(HEADS, rows, keys),
            shape(HEADS, rows, rows),
            shape(HEADS, keys, NOPE),
            shape(*do.shape),
            shape(*near.shape),
            shape(*far.shape),
        ],
        compiler_params=params(),
        cost_estimate=cost(9 * 10**9, 35 * 10**6),
        name="attend_main",
    )(spans, q, do, own, near, far, wk, wv, okv)


def call_tail(q, dos, own, near, far, wk, wv, ds, oe, k):
    rows = q.shape[0]
    keys = 3 * rows
    return pl.pallas_call(
        tail_body,
        grid=(HEADS // 2,),
        in_specs=[columns(rows, 2 * DQ), columns(rows, 2 * VDIM), whole(own), whole(near), whole(far),
                  columns(LATENT, 256), columns(LATENT, 256),
                  pairs(rows, keys), pairs(rows, rows), pairs(keys, NOPE)],
        out_specs=[columns(rows, 2 * DQ), whole(own)],
        scratch_shapes=[pltpu.VMEM((LATENT, rows), F32), pltpu.VMEM((ROPE, rows), F32)],
        out_shape=[shape(*q.shape), shape(*own.shape, dtype=F32)],
        compiler_params=params(),
        cost_estimate=cost(4 * 10**9, 30 * 10**6),
        name="attend_tail",
    )(q, dos, own, near, far, wk, wv, ds, oe, k)


def shifted(block, distance):
    n = lax.axis_size("ctx")
    return lax.ppermute(block, "ctx", [((i - distance) % n, i) for i in range(n)])


def on_device(queries, latent, w_key_up, w_value_up, grad_out, span_order):
    n = lax.axis_size("ctx")
    me = lax.axis_index("ctx")
    near = shifted(latent, 1)
    far = shifted(latent, 2)
    order = span_order.reshape(n, 2)
    spans = jnp.concatenate([order[(me - lag) % n] for lag in range(3)])
    okv = call_own_keys(latent, w_key_up, w_value_up)
    out, ds, oe, k, dos, t_near, t_far = call_main(
        spans, queries, grad_out, latent, near, far, w_key_up, w_value_up, okv
    )
    from_far = shifted(t_far, -2)
    from_near = shifted(t_near, -1)
    dq, own_term = call_tail(queries, dos, latent, near, far, w_key_up, w_value_up, ds, oe, k)
    total = own_term + from_near.astype(F32) + from_far.astype(F32)
    return out, dq, total.astype(BF)


def solution(mesh):
    rows = P(("dp", "ctx"), None)
    return jax.shard_map(
        on_device,
        mesh=mesh,
        in_specs=(rows, rows, P(), P(), rows, P("dp")),
        out_specs=(rows, rows, rows),
        check_vma=False,
    )
```

```python
import jax
import jax.numpy as jnp
from jax import lax
from jax.experimental import pallas as pl
from jax.experimental.pallas import tpu as pltpu
from jax.sharding import PartitionSpec as P

HEADS = 16
NOPE = 128
ROPE = 64
VDIM = 128
LATENT = 512
DQ = NOPE + ROPE
SCALE = DQ**-0.5
EXP2_SCALE = SCALE * 1.4426950408889634
MASKED = -1e30
NT = (((1,), (1,)), ((), ()))
TN = (((0,), (0,)), ((), ()))
F32 = jnp.float32
BF = jnp.bfloat16


def dot(x, y):
    return jnp.dot(x, y, preferred_element_type=F32)


def dot_rows(x, y):
    half = x.shape[0] // 2
    return jnp.concatenate([dot(x[:half], y), dot(x[half:], y)], 0)


def dot_nt(x, y):
    return lax.dot_general(x, y, NT, preferred_element_type=F32)


def dot_tn(x, y):
    return lax.dot_general(x, y, TN, preferred_element_type=F32)


def q_head(ref, h):
    return ref[:, h * DQ : (h + 1) * DQ]


def v_head(ref, h):
    return ref[:, h * VDIM : (h + 1) * VDIM]


def head_weights(wk_ref, wv_ref, h):
    return jnp.concatenate([v_head(wk_ref, h), v_head(wv_ref, h)], 1)


def positions(rows, spans):
    half = rows // 2
    last = len(spans) - 1
    col = lax.broadcasted_iota(jnp.int32, (1, half * len(spans)), 1)
    base = jnp.full(col.shape, (spans[last] - last) * half, jnp.int32)
    for j in range(last - 1, -1, -1):
        base = jnp.where(col < (j + 1) * half, (spans[j] - j) * half, base)
    return base + col


def keys_body(own, wk_ref, wv_ref, kv_ref):
    for h in range(2):
        kv_ref[h] = dot_rows(own[:, :LATENT], head_weights(wk_ref, wv_ref, h)).astype(BF)


def main_body(spans, q_ref, do_ref, own, near, far_a, far_b, wk_ref, wv_ref, okv_ref, nkv_ref,
              out_ref, ds_ref, oe_ref, fk_ref, dos_ref, tn_ref, tf_ref, bias, acc_t, rope_t, far, rope):
    p = pl.program_id(0)
    rows = q_ref.shape[0]
    half = rows // 2
    width = 2 * rows
    others = [spans[j] for j in range(2, 6)]
    pair = [spans[0], spans[1]]

    @pl.when(p == 0)
    def _():
        row = lax.broadcasted_iota(jnp.int32, (rows, 1), 0)
        q_pos = jnp.where(row < half, pair[0] * half, (pair[1] - 1) * half) + row
        far[...] = far_a[...] + far_b[...]
        rope[:rows] = near[:, LATENT:]
        rope[rows:width] = far[:, LATENT:]
        rope[width:] = own[:, LATENT:]
        bias[...] = jnp.where(positions(rows, pair) <= q_pos, 0.0, MASKED).astype(F32)
        acc_t[...] = jnp.zeros_like(acc_t)
        rope_t[...] = jnp.zeros_like(rope_t)

    other_pos = positions(rows, others)
    other_bias = [jnp.where(other_pos < pair[j] * half, 0.0, MASKED).astype(F32) for j in range(2)]
    def project(h):
        fkv = dot_rows(far[:, :LATENT], head_weights(wk_ref, wv_ref, h)).astype(BF)
        fk_ref[h] = fkv[:, :NOPE]
        kv = jnp.concatenate([nkv_ref[h], fkv, okv_ref[h]], 0)
        return jnp.concatenate([kv[:, :NOPE], rope[...]], 1), kv[:, NOPE:]

    def score(h, k):
        return dot_nt(q_head(q_ref, h), k)

    def soften(s):
        upper = s[:half, :width] + other_bias[0]
        lower = s[half:, :width] + other_bias[1]
        s = jnp.concatenate([jnp.concatenate([upper, lower], 0), s[:, width:] + bias[...]], 1)
        top = jnp.max(s, 1, keepdims=True)
        return jnp.exp2((s - top) * EXP2_SCALE).astype(BF)

    def attend(h, e, v):
        oe_ref[h] = e[:, width:]
        both = dot_rows(e, jnp.concatenate([v, jnp.ones_like(v)], 1))
        inv = 1.0 / both[:, VDIM:]
        out = both[:, :VDIM] * inv
        out_ref[:, h * VDIM : (h + 1) * VDIM] = out.astype(BF)
        dos = (v_head(do_ref, h).astype(F32) * inv).astype(BF)
        dos_ref[:, h * VDIM : (h + 1) * VDIM] = dos
        return dos, jnp.sum(out * dos.astype(F32), 1, keepdims=True)

    def dscores(h, e, dp, delta):
        ds = (e.astype(F32) * (dp - delta)).astype(BF)
        ds_ref[h] = ds
        return ds

    k0, v0 = project(0)
    k1, v1 = project(1)
    s0 = score(0, k0)
    s1 = score(1, k1)
    e0 = soften(s0)
    dos0, delta0 = attend(0, e0, v0)
    e1 = soften(s1)
    dp0 = dot_nt(dos0, v0)
    dos1, delta1 = attend(1, e1, v1)
    ds0 = dscores(0, e0, dp0, delta0)
    dp1 = dot_nt(dos1, v1)
    dv0 = dot_tn(dos0, e0[:, :width]).astype(BF)
    dk0 = dot_tn(q_head(q_ref, 0), ds0[:, :width]) * SCALE
    rope_t[...] += dk0[NOPE:]
    dk0 = dk0[:NOPE].astype(BF)
    ds1 = dscores(1, e1, dp1, delta1)
    dv1 = dot_tn(dos1, e1[:, :width]).astype(BF)
    dk1 = dot_tn(q_head(q_ref, 1), ds1[:, :width]) * SCALE
    rope_t[...] += dk1[NOPE:]
    dk1 = dk1[:NOPE].astype(BF)
    w = jnp.concatenate([wk_ref[:, 0*128:1*128+128], wv_ref[:, 0*128:1*128+128]], 1)
    acc_t[...] += dot(w, jnp.concatenate([dk0, dk1, dv0, dv1], 0))

    @pl.when(p == pl.num_programs(0) - 1)
    def _():
        tn_ref[:, :LATENT] = acc_t[:, :rows].astype(BF).T
        tn_ref[:, LATENT:] = rope_t[:, :rows].astype(BF).T
        tf_ref[:, :LATENT] = acc_t[:, rows:].astype(BF).T
        tf_ref[:, LATENT:] = rope_t[:, rows:].astype(BF).T


def tail_body(q_ref, dos_ref, own, near, far_a, far_b, wk_ref, wv_ref, ds_ref, oe_ref, nk_ref, fk_ref, ok_ref,
              dq_ref, t_ref, acc_t, rope_t, rope):
    p = pl.program_id(0)
    rows = q_ref.shape[0]
    width = 2 * rows

    @pl.when(p == 0)
    def _():
        rope[:rows] = near[:, LATENT:]
        rope[rows:width] = far_a[:, LATENT:] + far_b[:, LATENT:]
        rope[width:] = own[:, LATENT:]
        acc_t[...] = jnp.zeros_like(acc_t)
        rope_t[...] = jnp.zeros_like(rope_t)

    dqs, dks, dvs, rope_sum = [], [], [], None
    for h in range(2):
        ds = ds_ref[h]
        dv = dot_tn(v_head(dos_ref, h), oe_ref[h])
        dk = dot_tn(q_head(q_ref, h), ds[:, width:]) * SCALE
        dq = dot_rows(ds, jnp.concatenate([jnp.concatenate([nk_ref[h], fk_ref[h], ok_ref[h]], 0), rope[...]], 1)) * SCALE
        dqs.append(dq.astype(BF))
        dks.append(dk[:NOPE].astype(BF))
        dvs.append(dv.astype(BF))
        rope_sum = dk[NOPE:] if rope_sum is None else rope_sum + dk[NOPE:]
    dq_ref[...] = jnp.concatenate(dqs, 1)
    rope_t[...] += rope_sum
    w = jnp.concatenate([wk_ref[...], wv_ref[...]], 1)
    acc_t[...] += dot(w, jnp.concatenate(dks + dvs, 0))

    @pl.when(p == pl.num_programs(0) - 1)
    def _():
        t_ref[:, :LATENT] = acc_t[...].T
        t_ref[:, LATENT:] = rope_t[...].T


def whole(a):
    return pl.BlockSpec(a.shape, lambda p, *_: (0, 0))


def columns(rows, n):
    return pl.BlockSpec((rows, n), lambda p, *_: (0, p))


def pairs(rows, n):
    return pl.BlockSpec((2, rows, n), lambda p, *_: (p, 0, 0))


def params():
    return pltpu.CompilerParams(vmem_limit_bytes=48 * 2**20, dimension_semantics=("arbitrary",))


def cost(macs, size):
    return pl.CostEstimate(flops=2 * macs, bytes_accessed=size, transcendentals=0)


def shape(*dims, dtype=BF):
    return jax.ShapeDtypeStruct(dims, dtype)


def call_keys(own, wk, wv):
    rows = own.shape[0]
    return pl.pallas_call(
        keys_body,
        grid=(HEADS // 2,),
        in_specs=[whole(own), columns(LATENT, 256), columns(LATENT, 256)],
        out_specs=pairs(rows, 256),
        out_shape=shape(HEADS, rows, 256),
        compiler_params=params(),
        cost_estimate=cost(7 * 10**8, 8 * 10**6),
        name="project_keys",
    )(own, wk, wv)


def heads_block(n, rows, cols):
    return pl.BlockSpec((n, rows, cols), lambda p, *_: (p, 0, 0))


def call_main(spans, q, do, own, near, far_a, far_b, wk, wv, okv, nkv):
    rows = q.shape[0]
    keys = 3 * rows
    return pl.pallas_call(
        main_body,
        grid_spec=pltpu.PrefetchScalarGridSpec(
            num_scalar_prefetch=1,
            grid=(HEADS // 2,),
            in_specs=[columns(rows, 2 * DQ), columns(rows, 2 * VDIM), whole(own), whole(near), whole(near), whole(near),
                      columns(LATENT, 2 * 128), columns(LATENT, 2 * 128), heads_block(2, rows, 256), heads_block(2, rows, 256)],
            out_specs=[columns(rows, 2 * VDIM), heads_block(2, rows, keys), heads_block(2, rows, rows), heads_block(2, rows, NOPE),
                       columns(rows, 2 * VDIM), whole(near), whole(near)],
            scratch_shapes=[
                pltpu.VMEM((rows, rows), F32),
                pltpu.VMEM((LATENT, 2 * rows), F32),
                pltpu.VMEM((ROPE, 2 * rows), F32),
                pltpu.VMEM(near.shape, BF),
                pltpu.VMEM((keys, ROPE), BF),
            ],
        ),
        out_shape=[
            shape(*do.shape),
            shape(HEADS, rows, keys),
            shape(HEADS, rows, rows),
            shape(HEADS, rows, NOPE),
            shape(*do.shape),
            shape(*near.shape),
            shape(*near.shape),
        ],
        compiler_params=params(),
        cost_estimate=cost(9 * 10**9, 35 * 10**6),
        name="attend_main",
    )(spans, q, do, own, near, far_a, far_b, wk, wv, okv, nkv)


def call_tail(q, dos, own, near, far_a, far_b, wk, wv, ds, oe, nkv, fk, okv):
    rows = q.shape[0]
    keys = 3 * rows
    return pl.pallas_call(
        tail_body,
        grid=(HEADS // 2,),
        in_specs=[columns(rows, 2 * DQ), columns(rows, 2 * VDIM), whole(own), whole(near), whole(near), whole(near),
                  columns(LATENT, 256), columns(LATENT, 256),
                  pairs(rows, keys), pairs(rows, rows), pairs(rows, NOPE), pairs(rows, NOPE), pairs(rows, NOPE)],
        out_specs=[columns(rows, 2 * DQ), whole(own)],
        scratch_shapes=[pltpu.VMEM((LATENT, rows), F32), pltpu.VMEM((ROPE, rows), F32), pltpu.VMEM((keys, ROPE), BF)],
        out_shape=[shape(*q.shape), shape(*own.shape, dtype=F32)],
        compiler_params=params(),
        cost_estimate=cost(4 * 10**9, 30 * 10**6),
        name="attend_tail",
    )(q, dos, own, near, far_a, far_b, wk, wv, ds, oe, nkv, fk, okv)


def routed(block, distance, step=1):
    n = lax.axis_size("ctx")
    return lax.ppermute(block, "ctx", [((i - distance) % n, i) for i in range(0, n, step)])


def to_other_core(block):
    n = lax.axis_size("ctx")
    return lax.ppermute(block, "ctx", [(i, i + 1) for i in range(0, n, 2)])


def on_device(queries, latent, w_key_up, w_value_up, grad_out, span_order):
    n = lax.axis_size("ctx")
    me = lax.axis_index("ctx")
    near = routed(latent, 1)
    far_a = routed(latent, 2, 2)
    okv = call_keys(latent, w_key_up, w_value_up)
    near, okv = lax.optimization_barrier((near, okv))
    far_b = to_other_core(near)
    order = span_order.reshape(n, 2)
    spans = jnp.concatenate([order[(me - lag) % n] for lag in range(3)])
    nkv = call_keys(near, w_key_up, w_value_up)
    out, ds, oe, fk, dos, t_near, t_far = call_main(
        spans, queries, grad_out, latent, near, far_a, far_b, w_key_up, w_value_up, okv, nkv
    )
    from_far = routed(t_far, -2)
    from_near = routed(t_near, -1)
    dq, own_term = call_tail(
        queries, dos, latent, near, far_a, far_b, w_key_up, w_value_up, ds, oe, nkv, fk, okv
    )
    total = own_term + from_near.astype(F32) + from_far.astype(F32)
    return out, dq, total.astype(BF)


def solution(mesh):
    rows = P(("dp", "ctx"), None)
    return jax.shard_map(
        on_device,
        mesh=mesh,
        in_specs=(rows, rows, P(), P(), rows, P("dp")),
        out_specs=(rows, rows, rows),
        check_vma=False,
    )
```

```python
import jax
import jax.numpy as jnp
from jax import lax
from jax.experimental import pallas as pl
from jax.experimental.pallas import tpu as pltpu
from jax.sharding import PartitionSpec as P

HEADS = 16
NOPE = 128
ROPE = 64
VDIM = 128
LATENT = 512
DQ = NOPE + ROPE
SCALE = DQ**-0.5
EXP2_SCALE = SCALE * 1.4426950408889634
MASKED = -1e30
NT = (((1,), (1,)), ((), ()))
TN = (((0,), (0,)), ((), ()))
F32 = jnp.float32
BF = jnp.bfloat16


def dot(x, y):
    return jnp.dot(x, y, preferred_element_type=F32)


def dot_rows(x, y):
    half = x.shape[0] // 2
    return jnp.concatenate([dot(x[:half], y), dot(x[half:], y)], 0)


def dot_nt(x, y):
    return lax.dot_general(x, y, NT, preferred_element_type=F32)


def dot_tn(x, y):
    return lax.dot_general(x, y, TN, preferred_element_type=F32)


def q_head(ref, h):
    return ref[:, h * DQ : (h + 1) * DQ]


def v_head(ref, h):
    return ref[:, h * VDIM : (h + 1) * VDIM]


def head_weights(wk_ref, wv_ref, h):
    return jnp.concatenate([v_head(wk_ref, h), v_head(wv_ref, h)], 1)


def positions(rows, spans):
    half = rows // 2
    last = len(spans) - 1
    col = lax.broadcasted_iota(jnp.int32, (1, half * len(spans)), 1)
    base = jnp.full(col.shape, (spans[last] - last) * half, jnp.int32)
    for j in range(last - 1, -1, -1):
        base = jnp.where(col < (j + 1) * half, (spans[j] - j) * half, base)
    return base + col


def keys_body(own, wk_ref, wv_ref, kv_ref):
    w = jnp.concatenate([head_weights(wk_ref, wv_ref, h) for h in range(2)], 1)
    kv = dot(own[:, :LATENT], w).astype(BF)
    for h in range(2):
        kv_ref[h] = kv[:, h * 256 : (h + 1) * 256]


def main_body(spans, q_ref, do_ref, own, near, far_a, far_b, wk_ref, wv_ref, okv_ref,
              out_ref, dq_ref, ds_ref, oe_ref, dos_ref, tn_ref, tf_ref, bias, acc_t, rope_t, others_lat, rope, held_d, held_w):
    p = pl.program_id(0)
    rows = q_ref.shape[0]
    half = rows // 2
    width = 2 * rows
    others = [spans[j] for j in range(2, 6)]
    pair = [spans[0], spans[1]]

    @pl.when(p == 0)
    def _():
        row = lax.broadcasted_iota(jnp.int32, (rows, 1), 0)
        q_pos = jnp.where(row < half, pair[0] * half, (pair[1] - 1) * half) + row
        others_lat[:rows] = near[:, :LATENT]
        others_lat[rows:] = far_a[:, :LATENT] + far_b[:, :LATENT]
        rope[:rows] = near[:, LATENT:]
        rope[rows:width] = far_a[:, LATENT:] + far_b[:, LATENT:]
        rope[width:] = own[:, LATENT:]
        bias[...] = jnp.where(positions(rows, pair) <= q_pos, 0.0, MASKED).astype(F32)
        acc_t[...] = jnp.zeros_like(acc_t)
        held_d[...] = jnp.zeros_like(held_d)
        held_w[...] = jnp.zeros_like(held_w)
        rope_t[...] = jnp.zeros_like(rope_t)

    other_pos = positions(rows, others)
    other_bias = [jnp.where(other_pos < pair[j] * half, 0.0, MASKED).astype(F32) for j in range(2)]
    def project(h):
        kv = dot_rows(others_lat[...], head_weights(wk_ref, wv_ref, h)).astype(BF)
        kv = jnp.concatenate([kv, okv_ref[h]], 0)
        return jnp.concatenate([kv[:, :NOPE], rope[...]], 1), kv[:, NOPE:]

    def score(h, k):
        return dot_nt(q_head(q_ref, h), k)

    def soften(s):
        upper = s[:half, :width] + other_bias[0]
        lower = s[half:, :width] + other_bias[1]
        s = jnp.concatenate([jnp.concatenate([upper, lower], 0), s[:, width:] + bias[...]], 1)
        top = jnp.max(s, 1, keepdims=True)
        return jnp.exp2((s - top) * EXP2_SCALE).astype(BF)

    def attend(h, e, v):
        oe_ref[h] = e[:, width:]
        both = dot_rows(e, jnp.concatenate([v, jnp.ones_like(v)], 1))
        inv = 1.0 / both[:, VDIM:]
        out = both[:, :VDIM] * inv
        out_ref[:, h * VDIM : (h + 1) * VDIM] = out.astype(BF)
        dos = (v_head(do_ref, h).astype(F32) * inv).astype(BF)
        dos_ref[:, h * VDIM : (h + 1) * VDIM] = dos
        return dos, jnp.sum(out * dos.astype(F32), 1, keepdims=True)

    def dscores(h, e, dp, delta):
        ds = (e.astype(F32) * (dp - delta)).astype(BF)
        ds_ref[h] = ds[:, width:]
        return ds

    k0, v0 = project(0)
    k1, v1 = project(1)
    s0 = score(0, k0)
    s1 = score(1, k1)
    e0 = soften(s0)
    acc_t[: LATENT // 2] += dot(held_w[: LATENT // 2], held_d[...])
    dos0, delta0 = attend(0, e0, v0)
    e1 = soften(s1)
    acc_t[LATENT // 2 :] += dot(held_w[LATENT // 2 :], held_d[...])
    dp0 = dot_nt(dos0, v0)
    dos1, delta1 = attend(1, e1, v1)
    ds0 = dscores(0, e0, dp0, delta0)
    dp1 = dot_nt(dos1, v1)
    dv0 = dot_tn(dos0, e0[:, :width]).astype(BF)
    dk0 = dot_tn(q_head(q_ref, 0), ds0[:, :width]) * SCALE
    rope_t[...] += dk0[NOPE:]
    dk0 = dk0[:NOPE].astype(BF)
    dq0 = (dot_rows(ds0, k0) * SCALE).astype(BF)
    ds1 = dscores(1, e1, dp1, delta1)
    dv1 = dot_tn(dos1, e1[:, :width]).astype(BF)
    dk1 = dot_tn(q_head(q_ref, 1), ds1[:, :width]) * SCALE
    rope_t[...] += dk1[NOPE:]
    dk1 = dk1[:NOPE].astype(BF)
    dq1 = (dot_rows(ds1, k1) * SCALE).astype(BF)
    dq_ref[:, 0*DQ:(1+1)*DQ] = jnp.concatenate([dq0, dq1], 1)
    held_w[...] = jnp.concatenate([wk_ref[...], wv_ref[...]], 1)
    held_d[...] = jnp.concatenate([dk0, dk1, dv0, dv1], 0)

    @pl.when(p == pl.num_programs(0) - 1)
    def _():
        acc_t[...] += dot(held_w[...], held_d[...])
        tn_ref[:, :LATENT] = acc_t[:, :rows].astype(BF).T
        tn_ref[:, LATENT:] = rope_t[:, :rows].astype(BF).T
        tf_ref[:, :LATENT] = acc_t[:, rows:].astype(BF).T
        tf_ref[:, LATENT:] = rope_t[:, rows:].astype(BF).T


def tail_body(q_ref, dos_ref, wk_ref, wv_ref, ds_ref, oe_ref, t_ref, acc_t, rope_t):
    p = pl.program_id(0)

    @pl.when(p == 0)
    def _():
        acc_t[...] = jnp.zeros_like(acc_t)
        rope_t[...] = jnp.zeros_like(rope_t)

    heads = range(2)
    dvs = [dot_tn(v_head(dos_ref, h), oe_ref[h]).astype(BF) for h in heads]
    dks = [dot_tn(q_head(q_ref, h), ds_ref[h]) * SCALE for h in heads]
    rope_t[...] += dks[0][NOPE:] + dks[1][NOPE:]
    w = jnp.concatenate([wk_ref[...], wv_ref[...]], 1)
    acc_t[...] += dot(w, jnp.concatenate([dk[:NOPE].astype(BF) for dk in dks] + dvs, 0))

    @pl.when(p == pl.num_programs(0) - 1)
    def _():
        t_ref[:, :LATENT] = acc_t[...].T
        t_ref[:, LATENT:] = rope_t[...].T


def whole(a):
    return pl.BlockSpec(a.shape, lambda p, *_: (0, 0))


def columns(rows, n):
    return pl.BlockSpec((rows, n), lambda p, *_: (0, p))


def pairs(rows, n):
    return pl.BlockSpec((2, rows, n), lambda p, *_: (p, 0, 0))


def params():
    return pltpu.CompilerParams(vmem_limit_bytes=48 * 2**20, dimension_semantics=("arbitrary",))


def cost(macs, size):
    return pl.CostEstimate(flops=2 * macs, bytes_accessed=size, transcendentals=0)


def shape(*dims, dtype=BF):
    return jax.ShapeDtypeStruct(dims, dtype)


def call_keys(own, wk, wv):
    rows = own.shape[0]
    return pl.pallas_call(
        keys_body,
        grid=(HEADS // 2,),
        in_specs=[whole(own), columns(LATENT, 256), columns(LATENT, 256)],
        out_specs=pairs(rows, 256),
        out_shape=shape(HEADS, rows, 256),
        compiler_params=params(),
        cost_estimate=cost(7 * 10**8, 8 * 10**6),
        name="project_keys",
    )(own, wk, wv)


def heads_block(n, rows, cols):
    return pl.BlockSpec((n, rows, cols), lambda p, *_: (p, 0, 0))


def call_main(spans, q, do, own, near, far_a, far_b, wk, wv, okv):
    rows = q.shape[0]
    keys = 3 * rows
    return pl.pallas_call(
        main_body,
        grid_spec=pltpu.PrefetchScalarGridSpec(
            num_scalar_prefetch=1,
            grid=(HEADS // 2,),
            in_specs=[columns(rows, 2 * DQ), columns(rows, 2 * VDIM), whole(own), whole(near), whole(near), whole(near),
                      columns(LATENT, 2 * 128), columns(LATENT, 2 * 128), heads_block(2, rows, 256)],
            out_specs=[columns(rows, 2 * VDIM), columns(rows, 2 * DQ), heads_block(2, rows, rows), heads_block(2, rows, rows),
                       columns(rows, 2 * VDIM), whole(near), whole(near)],
            scratch_shapes=[
                pltpu.VMEM((rows, rows), F32),
                pltpu.VMEM((LATENT, 2 * rows), F32),
                pltpu.VMEM((ROPE, 2 * rows), F32),
                pltpu.VMEM((2 * rows, LATENT), BF),
                pltpu.VMEM((keys, ROPE), BF),
                pltpu.VMEM((4 * NOPE, 2 * rows), BF),
                pltpu.VMEM((LATENT, 4 * NOPE), BF),
            ],
        ),
        out_shape=[
            shape(*do.shape),
            shape(*q.shape),
            shape(HEADS, rows, rows),
            shape(HEADS, rows, rows),
            shape(*do.shape),
            shape(*near.shape),
            shape(*near.shape),
        ],
        compiler_params=params(),
        cost_estimate=cost(9 * 10**9, 35 * 10**6),
        name="attend_main",
    )(spans, q, do, own, near, far_a, far_b, wk, wv, okv)


def call_tail(q, dos, own, wk, wv, ds, oe):
    rows = q.shape[0]
    return pl.pallas_call(
        tail_body,
        grid=(HEADS // 2,),
        in_specs=[columns(rows, 2 * DQ), columns(rows, 2 * VDIM), columns(LATENT, 256), columns(LATENT, 256),
                  pairs(rows, rows), pairs(rows, rows)],
        out_specs=whole(own),
        scratch_shapes=[pltpu.VMEM((LATENT, rows), F32), pltpu.VMEM((ROPE, rows), F32)],
        out_shape=shape(*own.shape, dtype=F32),
        compiler_params=params(),
        cost_estimate=cost(3 * 10**9, 16 * 10**6),
        name="attend_tail",
    )(q, dos, wk, wv, ds, oe)


def routed(block, distance, step=1):
    n = lax.axis_size("ctx")
    return lax.ppermute(block, "ctx", [((i - distance) % n, i) for i in range(0, n, step)])


def to_other_core(block):
    n = lax.axis_size("ctx")
    return lax.ppermute(block, "ctx", [(i, i + 1) for i in range(0, n, 2)])


def on_device(queries, latent, w_key_up, w_value_up, grad_out, span_order):
    n = lax.axis_size("ctx")
    me = lax.axis_index("ctx")
    near = routed(latent, 1)
    far_a = routed(latent, 2, 2)
    okv = call_keys(latent, w_key_up, w_value_up)
    near, okv = lax.optimization_barrier((near, okv))
    far_b = to_other_core(near)
    order = span_order.reshape(n, 2)
    spans = jnp.concatenate([order[(me - lag) % n] for lag in range(3)])
    out, dq, ds, oe, dos, t_near, t_far = call_main(
        spans, queries, grad_out, latent, near, far_a, far_b, w_key_up, w_value_up, okv
    )
    from_far = routed(t_far, -2)
    from_near = routed(t_near, -1)
    own_term = call_tail(queries, dos, latent, w_key_up, w_value_up, ds, oe)
    total = own_term + from_near.astype(F32) + from_far.astype(F32)
    return out, dq, total.astype(BF)


def solution(mesh):
    rows = P(("dp", "ctx"), None)
    return jax.shard_map(
        on_device,
        mesh=mesh,
        in_specs=(rows, rows, P(), P(), rows, P("dp")),
        out_specs=(rows, rows, rows),
        check_vma=False,
    )
```

```python
import jax
import jax.numpy as jnp
from jax import lax
from jax.experimental import pallas as pl
from jax.experimental.pallas import tpu as pltpu
from jax.sharding import PartitionSpec as P

HEADS = 16
NOPE = 128
ROPE = 64
VDIM = 128
LATENT = 512
DQ = NOPE + ROPE
SCALE = DQ**-0.5
EXP2_SCALE = SCALE * 1.4426950408889634
MASKED = -1e30
NT = (((1,), (1,)), ((), ()))
TN = (((0,), (0,)), ((), ()))
F32 = jnp.float32
BF = jnp.bfloat16


def dot(x, y):
    return jnp.dot(x, y, preferred_element_type=F32)


def dot_rows(x, y):
    half = x.shape[0] // 2
    return jnp.concatenate([dot(x[:half], y), dot(x[half:], y)], 0)


def dot_nt(x, y):
    return lax.dot_general(x, y, NT, preferred_element_type=F32)


def dot_tn(x, y):
    return lax.dot_general(x, y, TN, preferred_element_type=F32)


def q_head(ref, h):
    return ref[:, h * DQ : (h + 1) * DQ]


def v_head(ref, h):
    return ref[:, h * VDIM : (h + 1) * VDIM]


def head_weights(wk_ref, wv_ref, h):
    return jnp.concatenate([v_head(wk_ref, h), v_head(wv_ref, h)], 1)


def positions(rows, spans):
    half = rows // 2
    last = len(spans) - 1
    col = lax.broadcasted_iota(jnp.int32, (1, half * len(spans)), 1)
    base = jnp.full(col.shape, (spans[last] - last) * half, jnp.int32)
    for j in range(last - 1, -1, -1):
        base = jnp.where(col < (j + 1) * half, (spans[j] - j) * half, base)
    return base + col


def keys_body(own, wk_ref, wv_ref, kv_ref):
    count = kv_ref.shape[0]
    w = jnp.concatenate([head_weights(wk_ref, wv_ref, h) for h in range(count)], 1)
    kv = dot(own[:, :LATENT], w).astype(BF)
    for h in range(count):
        kv_ref[h] = kv[:, h * 256 : (h + 1) * 256]


def pair_weights(wk_ref, wv_ref, j):
    cols = slice(j * 2 * NOPE, (j + 1) * 2 * NOPE)
    return jnp.concatenate([wk_ref[:, cols], wv_ref[:, cols]], 1)


def main_body(spans, q_ref, do_ref, own, near, far_a, far_b, wk_ref, wv_ref, okv_ref,
              out_ref, dq_ref, ds_ref, oe_ref, dos_ref, tn_ref, tf_ref, bias, acc_t, rope_t, others_lat, rope, held_d, held_w):
    p = pl.program_id(0)
    rows = q_ref.shape[0]
    half = rows // 2
    width = 2 * rows
    others = [spans[j] for j in range(2, 6)]
    pair = [spans[0], spans[1]]

    @pl.when(p == 0)
    def _():
        row = lax.broadcasted_iota(jnp.int32, (rows, 1), 0)
        q_pos = jnp.where(row < half, pair[0] * half, (pair[1] - 1) * half) + row
        others_lat[:rows] = near[:, :LATENT]
        others_lat[rows:] = far_a[:, :LATENT] + far_b[:, :LATENT]
        rope[:rows] = near[:, LATENT:]
        rope[rows:width] = far_a[:, LATENT:] + far_b[:, LATENT:]
        rope[width:] = own[:, LATENT:]
        bias[...] = jnp.where(positions(rows, pair) <= q_pos, 0.0, MASKED).astype(F32)
        acc_t[...] = jnp.zeros_like(acc_t)
        held_d[...] = jnp.zeros_like(held_d)
        held_w[...] = jnp.zeros_like(held_w)
        rope_t[...] = jnp.zeros_like(rope_t)

    other_pos = positions(rows, others)
    other_bias = [jnp.where(other_pos < pair[j] * half, 0.0, MASKED).astype(F32) for j in range(2)]
    def project(h):
        kv = dot_rows(others_lat[...], head_weights(wk_ref, wv_ref, h)).astype(BF)
        kv = jnp.concatenate([kv, okv_ref[h]], 0)
        return jnp.concatenate([kv[:, :NOPE], rope[...]], 1), kv[:, NOPE:]

    def score(h, k):
        return dot_nt(q_head(q_ref, h), k)

    def soften(s):
        upper = s[:half, :width] + other_bias[0]
        lower = s[half:, :width] + other_bias[1]
        s = jnp.concatenate([jnp.concatenate([upper, lower], 0), s[:, width:] + bias[...]], 1)
        top = jnp.max(s, 1, keepdims=True)
        return jnp.exp2((s - top) * EXP2_SCALE).astype(BF)

    def attend(h, e, v):
        oe_ref[h] = e[:, width:]
        both = dot_rows(e, jnp.concatenate([v, jnp.ones_like(v)], 1))
        inv = 1.0 / both[:, VDIM:]
        out = both[:, :VDIM] * inv
        out_ref[:, h * VDIM : (h + 1) * VDIM] = out.astype(BF)
        dos = (v_head(do_ref, h).astype(F32) * inv).astype(BF)
        dos_ref[:, h * VDIM : (h + 1) * VDIM] = dos
        return dos, jnp.sum(out * dos.astype(F32), 1, keepdims=True)

    def dscores(h, e, dp, delta):
        ds = (e.astype(F32) * (dp - delta)).astype(BF)
        ds_ref[h] = ds[:, width:]
        return ds

    k0, v0 = project(0)
    k1, v1 = project(1)
    s0 = score(0, k0)
    s1 = score(1, k1)
    e0 = soften(s0)
    acc_t[: LATENT // 2] += dot(held_w[: LATENT // 2], held_d[...])
    dos0, delta0 = attend(0, e0, v0)
    e1 = soften(s1)
    acc_t[LATENT // 2 :] += dot(held_w[LATENT // 2 :], held_d[...])
    dp0 = dot_nt(dos0, v0)
    dos1, delta1 = attend(1, e1, v1)
    ds0 = dscores(0, e0, dp0, delta0)
    dp1 = dot_nt(dos1, v1)
    dv0 = dot_tn(dos0, e0[:, :width]).astype(BF)
    dk0 = dot_tn(q_head(q_ref, 0), ds0[:, :width]) * SCALE
    rope_t[...] += dk0[NOPE:]
    dk0 = dk0[:NOPE].astype(BF)
    dq0 = (dot_rows(ds0, k0) * SCALE).astype(BF)
    ds1 = dscores(1, e1, dp1, delta1)
    dv1 = dot_tn(dos1, e1[:, :width]).astype(BF)
    dk1 = dot_tn(q_head(q_ref, 1), ds1[:, :width]) * SCALE
    rope_t[...] += dk1[NOPE:]
    dk1 = dk1[:NOPE].astype(BF)
    dq1 = (dot_rows(ds1, k1) * SCALE).astype(BF)
    dq_ref[:, 0*DQ:2*DQ] = jnp.concatenate([dq0, dq1], 1)
    k2, v2 = project(2)
    k3, v3 = project(3)
    s2 = score(2, k2)
    s3 = score(3, k3)
    e2 = soften(s2)
    w01 = pair_weights(wk_ref, wv_ref, 0)
    d01 = jnp.concatenate([dk0, dk1, dv0, dv1], 0)
    acc_t[: LATENT // 2] += dot(w01[: LATENT // 2], d01)
    dos2, delta2 = attend(2, e2, v2)
    e3 = soften(s3)
    acc_t[LATENT // 2 :] += dot(w01[LATENT // 2 :], d01)
    dp2 = dot_nt(dos2, v2)
    dos3, delta3 = attend(3, e3, v3)
    ds2 = dscores(2, e2, dp2, delta2)
    dp3 = dot_nt(dos3, v3)
    dv2 = dot_tn(dos2, e2[:, :width]).astype(BF)
    dk2 = dot_tn(q_head(q_ref, 2), ds2[:, :width]) * SCALE
    rope_t[...] += dk2[NOPE:]
    dk2 = dk2[:NOPE].astype(BF)
    dq2 = (dot_rows(ds2, k2) * SCALE).astype(BF)
    ds3 = dscores(3, e3, dp3, delta3)
    dv3 = dot_tn(dos3, e3[:, :width]).astype(BF)
    dk3 = dot_tn(q_head(q_ref, 3), ds3[:, :width]) * SCALE
    rope_t[...] += dk3[NOPE:]
    dk3 = dk3[:NOPE].astype(BF)
    dq3 = (dot_rows(ds3, k3) * SCALE).astype(BF)
    dq_ref[:, 2*DQ:4*DQ] = jnp.concatenate([dq2, dq3], 1)
    held_w[...] = pair_weights(wk_ref, wv_ref, 1)
    held_d[...] = jnp.concatenate([dk2, dk3, dv2, dv3], 0)

    @pl.when(p == pl.num_programs(0) - 1)
    def _():
        acc_t[...] += dot(held_w[...], held_d[...])
        tn_ref[:, :LATENT] = acc_t[:, :rows].astype(BF).T
        tn_ref[:, LATENT:] = rope_t[:, :rows].astype(BF).T
        tf_ref[:, :LATENT] = acc_t[:, rows:].astype(BF).T
        tf_ref[:, LATENT:] = rope_t[:, rows:].astype(BF).T


def tail_body(q_ref, dos_ref, wk_ref, wv_ref, ds_ref, oe_ref, t_ref, acc_t, rope_t, held_d, held_w):
    p = pl.program_id(0)
    count = ds_ref.shape[0]

    @pl.when(p == 0)
    def _():
        acc_t[...] = jnp.zeros_like(acc_t)
        rope_t[...] = jnp.zeros_like(rope_t)
        held_d[...] = jnp.zeros_like(held_d)
        held_w[...] = jnp.zeros_like(held_w)

    dvs = [dot_tn(v_head(dos_ref, h), oe_ref[h]).astype(BF) for h in range(count)]
    dks = [dot_tn(q_head(q_ref, h), ds_ref[h]) * SCALE for h in range(count)]
    rope_t[...] += sum(dk[NOPE:] for dk in dks)
    w = jnp.concatenate([wk_ref[...], wv_ref[...]], 1)
    acc_t[...] += dot(w, jnp.concatenate([dk[:NOPE].astype(BF) for dk in dks] + dvs, 0))

    @pl.when(p == pl.num_programs(0) - 1)
    def _():
        t_ref[:, :LATENT] = acc_t[...].T
        t_ref[:, LATENT:] = rope_t[...].T


def whole(a):
    return pl.BlockSpec(a.shape, lambda p, *_: (0, 0))


def columns(rows, n):
    return pl.BlockSpec((rows, n), lambda p, *_: (0, p))


def pairs(rows, n):
    return pl.BlockSpec((2, rows, n), lambda p, *_: (p, 0, 0))


def params():
    return pltpu.CompilerParams(vmem_limit_bytes=48 * 2**20, dimension_semantics=("arbitrary",))


def cost(macs, size):
    return pl.CostEstimate(flops=2 * macs, bytes_accessed=size, transcendentals=0)


def shape(*dims, dtype=BF):
    return jax.ShapeDtypeStruct(dims, dtype)


def call_keys(own, wk, wv):
    rows = own.shape[0]
    return pl.pallas_call(
        keys_body,
        grid=(HEADS // 4,),
        in_specs=[whole(own), columns(LATENT, 4 * NOPE), columns(LATENT, 4 * NOPE)],
        out_specs=heads_block(4, rows, 256),
        out_shape=shape(HEADS, rows, 256),
        compiler_params=params(),
        cost_estimate=cost(7 * 10**8, 8 * 10**6),
        name="project_keys",
    )(own, wk, wv)


def heads_block(n, rows, cols):
    return pl.BlockSpec((n, rows, cols), lambda p, *_: (p, 0, 0))


def call_main(spans, q, do, own, near, far_a, far_b, wk, wv, okv):
    rows = q.shape[0]
    keys = 3 * rows
    return pl.pallas_call(
        main_body,
        grid_spec=pltpu.PrefetchScalarGridSpec(
            num_scalar_prefetch=1,
            grid=(HEADS // 4,),
            in_specs=[columns(rows, 4 * DQ), columns(rows, 4 * VDIM), whole(own), whole(near), whole(near), whole(near),
                      columns(LATENT, 4 * NOPE), columns(LATENT, 4 * NOPE), heads_block(4, rows, 256)],
            out_specs=[columns(rows, 4 * VDIM), columns(rows, 4 * DQ), heads_block(4, rows, rows), heads_block(4, rows, rows),
                       columns(rows, 4 * VDIM), whole(near), whole(near)],
            scratch_shapes=[
                pltpu.VMEM((rows, rows), F32),
                pltpu.VMEM((LATENT, 2 * rows), F32),
                pltpu.VMEM((ROPE, 2 * rows), F32),
                pltpu.VMEM((2 * rows, LATENT), BF),
                pltpu.VMEM((keys, ROPE), BF),
                pltpu.VMEM((4 * NOPE, 2 * rows), BF),
                pltpu.VMEM((LATENT, 4 * NOPE), BF),
            ],
        ),
        out_shape=[
            shape(*do.shape),
            shape(*q.shape),
            shape(HEADS, rows, rows),
            shape(HEADS, rows, rows),
            shape(*do.shape),
            shape(*near.shape),
            shape(*near.shape),
        ],
        compiler_params=params(),
        cost_estimate=cost(9 * 10**9, 35 * 10**6),
        name="attend_main",
    )(spans, q, do, own, near, far_a, far_b, wk, wv, okv)


def call_tail(q, dos, own, wk, wv, ds, oe):
    rows = q.shape[0]
    return pl.pallas_call(
        tail_body,
        grid=(HEADS // 4,),
        in_specs=[columns(rows, 4 * DQ), columns(rows, 4 * VDIM), columns(LATENT, 4 * NOPE), columns(LATENT, 4 * NOPE),
                  heads_block(4, rows, rows), heads_block(4, rows, rows)],
        out_specs=whole(own),
        scratch_shapes=[pltpu.VMEM((LATENT, rows), F32), pltpu.VMEM((ROPE, rows), F32),
                        pltpu.VMEM((8 * NOPE, rows), BF), pltpu.VMEM((LATENT, 8 * NOPE), BF)],
        out_shape=shape(*own.shape, dtype=F32),
        compiler_params=params(),
        cost_estimate=cost(3 * 10**9, 16 * 10**6),
        name="attend_tail",
    )(q, dos, wk, wv, ds, oe)


def routed(block, distance, step=1):
    n = lax.axis_size("ctx")
    return lax.ppermute(block, "ctx", [((i - distance) % n, i) for i in range(0, n, step)])


def to_other_core(block):
    n = lax.axis_size("ctx")
    return lax.ppermute(block, "ctx", [(i, i + 1) for i in range(0, n, 2)])


def on_device(queries, latent, w_key_up, w_value_up, grad_out, span_order):
    n = lax.axis_size("ctx")
    me = lax.axis_index("ctx")
    near = routed(latent, 1)
    far_a = routed(latent, 2, 2)
    okv = call_keys(latent, w_key_up, w_value_up)
    near, okv = lax.optimization_barrier((near, okv))
    far_b = to_other_core(near)
    order = span_order.reshape(n, 2)
    spans = jnp.concatenate([order[(me - lag) % n] for lag in range(3)])
    out, dq, ds, oe, dos, t_near, t_far = call_main(
        spans, queries, grad_out, latent, near, far_a, far_b, w_key_up, w_value_up, okv
    )
    from_far = routed(t_far, -2)
    from_near = routed(t_near, -1)
    own_term = call_tail(queries, dos, latent, w_key_up, w_value_up, ds, oe)
    total = own_term + from_near.astype(F32) + from_far.astype(F32)
    return out, dq, total.astype(BF)


def solution(mesh):
    rows = P(("dp", "ctx"), None)
    return jax.shard_map(
        on_device,
        mesh=mesh,
        in_specs=(rows, rows, P(), P(), rows, P("dp")),
        out_specs=(rows, rows, rows),
        check_vma=False,
    )
```

```python
import jax
import jax.numpy as jnp
from jax import lax
from jax.experimental import pallas as pl
from jax.experimental.pallas import tpu as pltpu
from jax.sharding import PartitionSpec as P

HEADS = 16
NOPE = 128
ROPE = 64
VDIM = 128
LATENT = 512
DQ = NOPE + ROPE
SCALE = DQ**-0.5
EXP2_SCALE = SCALE * 1.4426950408889634
MASKED = -1e30
NT = (((1,), (1,)), ((), ()))
TN = (((0,), (0,)), ((), ()))
F32 = jnp.float32
BF = jnp.bfloat16


def dot(x, y):
    return jnp.dot(x, y, preferred_element_type=F32)


def dot_rows(x, y):
    half = x.shape[0] // 2
    return jnp.concatenate([dot(x[:half], y), dot(x[half:], y)], 0)


def dot_nt(x, y):
    return lax.dot_general(x, y, NT, preferred_element_type=F32)


def dot_tn(x, y):
    return lax.dot_general(x, y, TN, preferred_element_type=F32)


def q_head(ref, h):
    return ref[:, h * DQ : (h + 1) * DQ]


def v_head(ref, h):
    return ref[:, h * VDIM : (h + 1) * VDIM]


def head_weights(wk_ref, wv_ref, h):
    return jnp.concatenate([v_head(wk_ref, h), v_head(wv_ref, h)], 1)


def positions(rows, spans):
    half = rows // 2
    last = len(spans) - 1
    col = lax.broadcasted_iota(jnp.int32, (1, half * len(spans)), 1)
    base = jnp.full(col.shape, (spans[last] - last) * half, jnp.int32)
    for j in range(last - 1, -1, -1):
        base = jnp.where(col < (j + 1) * half, (spans[j] - j) * half, base)
    return base + col


def keys_body(own, wk_ref, wv_ref, kv_ref):
    count = kv_ref.shape[0]
    w = jnp.concatenate([head_weights(wk_ref, wv_ref, h) for h in range(count)], 1)
    kv = dot(own[:, :LATENT], w).astype(BF)
    for h in range(count):
        kv_ref[h] = kv[:, h * 256 : (h + 1) * 256]


def pair_weights(wk_ref, wv_ref, j):
    cols = slice(j * 2 * NOPE, (j + 1) * 2 * NOPE)
    return jnp.concatenate([wk_ref[:, cols], wv_ref[:, cols]], 1)


def main_body(spans, q_ref, do_ref, own, near, far_a, far_b, wk_ref, wv_ref, okv_ref,
              out_ref, dq_ref, ds_ref, oe_ref, dos_ref, tn_ref, tf_ref, bias, acc_t, rope_t, others_lat, rope, held_d, held_w):
    p = pl.program_id(0)
    rows = q_ref.shape[0]
    half = rows // 2
    width = 2 * rows
    others = [spans[j] for j in range(2, 6)]
    pair = [spans[0], spans[1]]

    @pl.when(p == 0)
    def _():
        row = lax.broadcasted_iota(jnp.int32, (rows, 1), 0)
        q_pos = jnp.where(row < half, pair[0] * half, (pair[1] - 1) * half) + row
        others_lat[:rows] = near[:, :LATENT]
        others_lat[rows:] = far_a[:, :LATENT] + far_b[:, :LATENT]
        rope[:rows] = near[:, LATENT:]
        rope[rows:width] = far_a[:, LATENT:] + far_b[:, LATENT:]
        rope[width:] = own[:, LATENT:]
        bias[...] = jnp.where(positions(rows, pair) <= q_pos, 0.0, MASKED).astype(F32)
        acc_t[...] = jnp.zeros_like(acc_t)
        held_d[...] = jnp.zeros_like(held_d)
        held_w[...] = jnp.zeros_like(held_w)
        rope_t[...] = jnp.zeros_like(rope_t)

    other_pos = positions(rows, others)
    other_bias = [jnp.where(other_pos < pair[j] * half, 0.0, MASKED).astype(F32) for j in range(2)]
    def project(h):
        kv = dot_rows(others_lat[...], head_weights(wk_ref, wv_ref, h)).astype(BF)
        kv = jnp.concatenate([kv, okv_ref[h]], 0)
        return jnp.concatenate([kv[:, :NOPE], rope[...]], 1), kv[:, NOPE:]

    def score(h, k):
        return dot_nt(q_head(q_ref, h), k)

    def soften(s):
        upper = s[:half, :width] + other_bias[0]
        lower = s[half:, :width] + other_bias[1]
        s = jnp.concatenate([jnp.concatenate([upper, lower], 0), s[:, width:] + bias[...]], 1)
        top = jnp.max(s, 1, keepdims=True)
        return jnp.exp2((s - top) * EXP2_SCALE).astype(BF)

    def attend(h, e, v):
        oe_ref[h] = e[:, width:]
        both = dot_rows(e, jnp.concatenate([v, jnp.ones_like(v)], 1))
        inv = 1.0 / both[:, VDIM:]
        out = both[:, :VDIM] * inv
        out_ref[:, h * VDIM : (h + 1) * VDIM] = out.astype(BF)
        dos = (v_head(do_ref, h).astype(F32) * inv).astype(BF)
        dos_ref[:, h * VDIM : (h + 1) * VDIM] = dos
        return dos, jnp.sum(out * dos.astype(F32), 1, keepdims=True)

    def dscores(h, e, dp, delta):
        ds = (e.astype(F32) * (dp - delta)).astype(BF)
        ds_ref[h] = ds[:, width:]
        return ds

    k0, v0 = project(0)
    k1, v1 = project(1)
    s0 = score(0, k0)
    s1 = score(1, k1)
    e0 = soften(s0)
    acc_t[: LATENT // 2] += dot(held_w[: LATENT // 2], held_d[...])
    dos0, delta0 = attend(0, e0, v0)
    e1 = soften(s1)
    acc_t[LATENT // 2 :] += dot(held_w[LATENT // 2 :], held_d[...])
    dp0 = dot_nt(dos0, v0)
    dos1, delta1 = attend(1, e1, v1)
    ds0 = dscores(0, e0, dp0, delta0)
    dp1 = dot_nt(dos1, v1)
    dv0 = dot_tn(dos0, e0[:, :width]).astype(BF)
    dk0 = dot_tn(q_head(q_ref, 0), ds0[:, :width]) * SCALE
    rope_t[...] += dk0[NOPE:]
    dk0 = dk0[:NOPE].astype(BF)
    dq0 = (dot_rows(ds0, k0) * SCALE).astype(BF)
    ds1 = dscores(1, e1, dp1, delta1)
    dv1 = dot_tn(dos1, e1[:, :width]).astype(BF)
    dk1 = dot_tn(q_head(q_ref, 1), ds1[:, :width]) * SCALE
    rope_t[...] += dk1[NOPE:]
    dk1 = dk1[:NOPE].astype(BF)
    dq1 = (dot_rows(ds1, k1) * SCALE).astype(BF)
    dq_ref[:, 0*DQ:2*DQ] = jnp.concatenate([dq0, dq1], 1)
    k2, v2 = project(2)
    k3, v3 = project(3)
    s2 = score(2, k2)
    s3 = score(3, k3)
    e2 = soften(s2)
    w01 = pair_weights(wk_ref, wv_ref, 0)
    d01 = jnp.concatenate([dk0, dk1, dv0, dv1], 0)
    acc_t[: LATENT // 2] += dot(w01[: LATENT // 2], d01)
    dos2, delta2 = attend(2, e2, v2)
    e3 = soften(s3)
    acc_t[LATENT // 2 :] += dot(w01[LATENT // 2 :], d01)
    dp2 = dot_nt(dos2, v2)
    dos3, delta3 = attend(3, e3, v3)
    ds2 = dscores(2, e2, dp2, delta2)
    dp3 = dot_nt(dos3, v3)
    dv2 = dot_tn(dos2, e2[:, :width]).astype(BF)
    dk2 = dot_tn(q_head(q_ref, 2), ds2[:, :width]) * SCALE
    rope_t[...] += dk2[NOPE:]
    dk2 = dk2[:NOPE].astype(BF)
    dq2 = (dot_rows(ds2, k2) * SCALE).astype(BF)
    ds3 = dscores(3, e3, dp3, delta3)
    dv3 = dot_tn(dos3, e3[:, :width]).astype(BF)
    dk3 = dot_tn(q_head(q_ref, 3), ds3[:, :width]) * SCALE
    rope_t[...] += dk3[NOPE:]
    dk3 = dk3[:NOPE].astype(BF)
    dq3 = (dot_rows(ds3, k3) * SCALE).astype(BF)
    dq_ref[:, 2*DQ:4*DQ] = jnp.concatenate([dq2, dq3], 1)
    held_w[...] = pair_weights(wk_ref, wv_ref, 1)
    held_d[...] = jnp.concatenate([dk2, dk3, dv2, dv3], 0)

    @pl.when(p == pl.num_programs(0) - 1)
    def _():
        acc_t[...] += dot(held_w[...], held_d[...])
        tn_ref[:, :LATENT] = acc_t[:, :rows].astype(BF).T
        tn_ref[:, LATENT:] = rope_t[:, :rows].astype(BF).T
        tf_ref[:, :LATENT] = acc_t[:, rows:].astype(BF).T
        tf_ref[:, LATENT:] = rope_t[:, rows:].astype(BF).T


def tail_body(q_ref, dos_ref, wk_ref, wv_ref, ds_ref, oe_ref, t_ref, acc_t, rope_t, held_d, held_w):
    p = pl.program_id(0)
    count = ds_ref.shape[0]

    @pl.when(p == 0)
    def _():
        acc_t[...] = jnp.zeros_like(acc_t)
        rope_t[...] = jnp.zeros_like(rope_t)
        held_d[...] = jnp.zeros_like(held_d)
        held_w[...] = jnp.zeros_like(held_w)

    dvs = [dot_tn(v_head(dos_ref, h), oe_ref[h]).astype(BF) for h in range(count)]
    dks = [dot_tn(q_head(q_ref, h), ds_ref[h]) * SCALE for h in range(count)]
    rope_t[...] += sum(dk[NOPE:] for dk in dks)
    w = jnp.concatenate([wk_ref[...], wv_ref[...]], 1)
    acc_t[...] += dot(w, jnp.concatenate([dk[:NOPE].astype(BF) for dk in dks] + dvs, 0))

    @pl.when(p == pl.num_programs(0) - 1)
    def _():
        t_ref[:, :LATENT] = acc_t[...].T
        t_ref[:, LATENT:] = rope_t[...].T


def whole(a):
    return pl.BlockSpec(a.shape, lambda p, *_: (0, 0))


def columns(rows, n):
    return pl.BlockSpec((rows, n), lambda p, *_: (0, p))


def pairs(rows, n):
    return pl.BlockSpec((2, rows, n), lambda p, *_: (p, 0, 0))


def params():
    return pltpu.CompilerParams(vmem_limit_bytes=48 * 2**20, dimension_semantics=("arbitrary",))


def cost(macs, size):
    return pl.CostEstimate(flops=2 * macs, bytes_accessed=size, transcendentals=0)


def shape(*dims, dtype=BF):
    return jax.ShapeDtypeStruct(dims, dtype)


def call_keys(own, wk, wv):
    rows = own.shape[0]
    return pl.pallas_call(
        keys_body,
        grid=(HEADS // 4,),
        in_specs=[whole(own), columns(LATENT, 4 * NOPE), columns(LATENT, 4 * NOPE)],
        out_specs=heads_block(4, rows, 256),
        out_shape=shape(HEADS, rows, 256),
        compiler_params=params(),
        cost_estimate=cost(7 * 10**8, 8 * 10**6),
        name="project_keys",
    )(own, wk, wv)


def heads_block(n, rows, cols):
    return pl.BlockSpec((n, rows, cols), lambda p, *_: (p, 0, 0))


def call_main(spans, q, do, own, near, far_a, far_b, wk, wv, okv):
    rows = q.shape[0]
    keys = 3 * rows
    return pl.pallas_call(
        main_body,
        grid_spec=pltpu.PrefetchScalarGridSpec(
            num_scalar_prefetch=1,
            grid=(HEADS // 4,),
            in_specs=[columns(rows, 4 * DQ), columns(rows, 4 * VDIM), whole(own), whole(near), whole(near), whole(near),
                      columns(LATENT, 4 * NOPE), columns(LATENT, 4 * NOPE), heads_block(4, rows, 256)],
            out_specs=[columns(rows, 4 * VDIM), columns(rows, 4 * DQ), heads_block(4, rows, rows), heads_block(4, rows, rows),
                       columns(rows, 4 * VDIM), whole(near), whole(near)],
            scratch_shapes=[
                pltpu.VMEM((rows, rows), F32),
                pltpu.VMEM((LATENT, 2 * rows), F32),
                pltpu.VMEM((ROPE, 2 * rows), F32),
                pltpu.VMEM((2 * rows, LATENT), BF),
                pltpu.VMEM((keys, ROPE), BF),
                pltpu.VMEM((4 * NOPE, 2 * rows), BF),
                pltpu.VMEM((LATENT, 4 * NOPE), BF),
            ],
        ),
        out_shape=[
            shape(*do.shape),
            shape(*q.shape),
            shape(HEADS, rows, rows),
            shape(HEADS, rows, rows),
            shape(*do.shape),
            shape(*near.shape),
            shape(*near.shape),
        ],
        compiler_params=params(),
        cost_estimate=cost(9 * 10**9, 35 * 10**6),
        name="attend_main",
    )(spans, q, do, own, near, far_a, far_b, wk, wv, okv)


def call_tail(q, dos, own, wk, wv, ds, oe):
    rows = q.shape[0]
    return pl.pallas_call(
        tail_body,
        grid=(HEADS // 4,),
        in_specs=[columns(rows, 4 * DQ), columns(rows, 4 * VDIM), columns(LATENT, 4 * NOPE), columns(LATENT, 4 * NOPE),
                  heads_block(4, rows, rows), heads_block(4, rows, rows)],
        out_specs=whole(own),
        scratch_shapes=[pltpu.VMEM((LATENT, rows), F32), pltpu.VMEM((ROPE, rows), F32),
                        pltpu.VMEM((8 * NOPE, rows), BF), pltpu.VMEM((LATENT, 8 * NOPE), BF)],
        out_shape=shape(*own.shape, dtype=F32),
        compiler_params=params(),
        cost_estimate=cost(3 * 10**9, 16 * 10**6),
        name="attend_tail",
    )(q, dos, wk, wv, ds, oe)


def routed(block, distance, step=1):
    n = lax.axis_size("ctx")
    return lax.ppermute(block, "ctx", [((i - distance) % n, i) for i in range(0, n, step)])


def to_other_core(block):
    n = lax.axis_size("ctx")
    return lax.ppermute(block, "ctx", [(i, i + 1) for i in range(0, n, 2)])


def on_device(queries, latent, w_key_up, w_value_up, grad_out, span_order):
    n = lax.axis_size("ctx")
    me = lax.axis_index("ctx")
    near = routed(latent, 1)
    far_a = routed(latent, 2, 2)
    okv = call_keys(latent, w_key_up, w_value_up)
    near, okv = lax.optimization_barrier((near, okv))
    far_b = to_other_core(near)
    order = span_order.reshape(n, 2)
    spans = jnp.concatenate([order[(me - lag) % n] for lag in range(3)])
    out, dq, ds, oe, dos, t_near, t_far = call_main(
        spans, queries, grad_out, latent, near, far_a, far_b, w_key_up, w_value_up, okv
    )
    swapped = lax.ppermute(t_near, "ctx", [(i, i ^ 1) for i in range(n)])
    odd = me % 2 == 1
    none = jnp.zeros_like(swapped)
    passed_on, ds = lax.optimization_barrier((t_far + jnp.where(odd, swapped, none), ds))
    arrived = routed(passed_on, -2)
    own_term = call_tail(queries, dos, latent, w_key_up, w_value_up, ds, oe)
    total = own_term + arrived.astype(F32) + jnp.where(odd, none, swapped).astype(F32)
    return out, dq, total.astype(BF)


def solution(mesh):
    rows = P(("dp", "ctx"), None)
    return jax.shard_map(
        on_device,
        mesh=mesh,
        in_specs=(rows, rows, P(), P(), rows, P("dp")),
        out_specs=(rows, rows, rows),
        check_vma=False,
    )
```
